32 devices in a mesh: owner: 4 (over x, core), fsdp: 8 (over z, y).
Axes of the slice: x: 2, y: 2, z: 4, core: 2. Of those that a mesh axis runs over, the one named last changes fastest.
Arguments:
- precond: bfloat16 [4, 2048, 2048], P('owner', 'fsdp'), as said below
- basis_old: bfloat16 [4, 2048, 2048], P('owner', 'fsdp'), as said below
- gradient: bfloat16 [8192, 8192], P('owner', 'fsdp'), may hold values from -6 to 6
- moment_in: float32 [8192, 8192], P('owner', 'fsdp')
- second_in: float32 [8192, 8192], P('owner', 'fsdp'), may hold values from 0.3 to 3
Outputs:
- update: bfloat16 [8192, 8192], P('owner', 'fsdp')
- moment_one: float32 [8192, 8192], P('owner', 'fsdp')
- moment_two: float32 [8192, 8192], P('owner', 'fsdp')
- basis_new: float32 [4, 2048, 2048], P('owner', 'fsdp')
The draws below stay inside these ranges and needn't reach their ends.
Inputs may be any that keep to these rules, and one draw needn't show every extreme that they name: Each block of precond is symmetric and positive definite. Each block of basis_old is invertible.
All inputs are finite; a program needn't handle non-finite values.
Results may differ from the reference program's by a relative error of at most 0.024.
Values may be sent and summed in bfloat16 or wider, within the bound.
A program may use at most 192 MiB of HBM per device.

```python
import math
import jax
import jax.numpy as jnp
from jax import lax

D = 8192
B = 2048
NBLK = 4
ROWS = 8192


def draw_precond(key, part):
    key = jax.random.fold_in(key, 11)
    first, second, third = jax.random.split(key, 3)
    noise = jax.random.normal(first, (NBLK, B, B), jnp.float32)
    symmetric = (noise + jnp.swapaxes(noise, 1, 2)) * (1.0 / jnp.sqrt(2.0 * B))
    diagonal = jnp.exp(jax.random.uniform(second, (NBLK, B), jnp.float32, jnp.log(3.0), jnp.log(6.0)))
    direction = jnp.abs(jax.random.normal(third, (NBLK, B), jnp.float32)) * (1.0 / jnp.sqrt(1.0 * B))
    spike = 20.0 * direction[:, :, None] * direction[:, None, :]
    eye_full = jnp.eye(B, dtype=jnp.float32)
    return (symmetric + spike + eye_full[None, :, :] * diagonal[:, :, None]).astype(jnp.bfloat16)


def draw_basis_old(key, part):
    key = jax.random.fold_in(key, 23)
    noise = jax.random.normal(key, (NBLK, B, B), jnp.float32)
    eye_full = jnp.eye(B, dtype=jnp.float32)
    return (eye_full[None, :, :] + 0.3 * noise / jnp.sqrt(1.0 * B)).astype(jnp.bfloat16)


def draw_moment_in(key, part):
    key = jax.random.fold_in(key, 37)
    first, second, third = jax.random.split(key, 3)
    row_pos = jnp.arange(ROWS, dtype=jnp.float32) / max(ROWS - 1, 1)
    col_pos = jnp.arange(D, dtype=jnp.float32) / max(D - 1, 1)
    rough_rows = jnp.exp(jax.random.uniform(second, (ROWS, 1), jnp.float32, -0.25, 0.25))
    rough_cols = jnp.exp(jax.random.uniform(third, (1, D), jnp.float32, -0.25, 0.25))
    row_ramp = 3.0 ** row_pos
    col_ramp = 3.0 ** col_pos
    noise = jax.random.normal(first, (ROWS, D), jnp.float32)
    values = 0.3 * row_ramp[:, None] * col_ramp[None, :] * rough_rows * rough_cols * noise
    return values.astype(jnp.float32)


def block_levels(rng, extent, pieces, smallest, high):
    def one(position, shards_of):
        heights = jax.random.uniform(jax.random.fold_in(jax.random.fold_in(rng, 6), position), (shards_of,), jnp.float32, smallest / len(pieces), high / len(pieces))
        return jnp.repeat(jnp.exp(heights), extent[position] // shards_of).reshape((-1,) + (1,) * (len(extent) - position - 1))

    level = one(*pieces[0])
    for cut in pieces[1:]:
        level = level * one(*cut)
    return level


def centred(stream_key, dims, spread, reach, cuts=(), kind=jnp.bfloat16):
    drawn = jax.random.normal(stream_key, dims, jnp.float32) * spread
    if len(cuts) > 0:
        drawn = block_levels(stream_key, dims, cuts, -0.22, 0.18) * drawn
    return jnp.clip(drawn, min=-reach, max=reach).astype(kind)


def setup_inputs(seed: int = 0) -> dict:
    key_list = jax.random.split(jax.random.key(seed), 6)
    precond = draw_precond(jax.random.fold_in(key_list[5], 71), 0)
    basis_old = draw_basis_old(jax.random.fold_in(key_list[5], 71), 0)
    gradient = centred(key_list[2], (ROWS, D), 1.0, 6.0, ((0, 4), (1, 8)))
    moment_in = draw_moment_in(jax.random.fold_in(key_list[5], 71), 0)
    second_in = jnp.clip(jnp.exp(math.log(3.0) - 2.3025851 * jax.random.uniform(key_list[4], (ROWS, D), jnp.float32) ** block_levels(key_list[4], (ROWS, D), ((0, 4), (1, 8)), -0.2, 0.2)), 0.3, 3.0)
    return dict(precond=precond, basis_old=basis_old, gradient=gradient, moment_in=moment_in, second_in=second_in)


beta_one = 0.9
beta_two = 0.95
small_eps = 1e-08
norm_eps = 1e-06

def orthonormal(chol, power):

    def solve_one(factor, rows):
        return jax.scipy.linalg.solve_triangular(factor, rows.T, lower=True).T
    return jax.vmap(solve_one)(chol, power)

def reference(precond, basis_old, gradient, moment_in, second_in):
    upper_limit = lax.Precision.HIGHEST
    power = jnp.einsum('bik,bkj->bij', precond.astype(jnp.float32), basis_old.astype(jnp.float32), precision=upper_limit)
    power_half = lax.optimization_barrier(power.astype(jnp.bfloat16))
    power_wide = power_half.astype(jnp.float32)
    gram_sum = jnp.einsum('bki,bkj->bij', power_wide, power_wide, precision=upper_limit)
    chol = jnp.linalg.cholesky(gram_sum)
    basis_new = orthonormal(chol, power_wide)
    basis_half = basis_new.astype(jnp.bfloat16)
    moment_one = beta_one * moment_in + (1.0 - beta_one) * gradient.astype(jnp.float32)
    moment_half = moment_one.astype(jnp.bfloat16)
    broad_basis_matrix = basis_half.astype(jnp.float32)
    gradient_block_list = gradient.reshape(NBLK, B, D).astype(jnp.float32)
    moment_block_list = moment_half.reshape(NBLK, B, D).astype(jnp.float32)
    rotated_gradient = jnp.einsum('aos,aol->asl', broad_basis_matrix, gradient_block_list, precision=upper_limit)
    rotated_moment = jnp.einsum('aos,aol->asl', broad_basis_matrix, moment_block_list, precision=upper_limit)
    moment_two = beta_two * second_in + (1.0 - beta_two) * jnp.square(rotated_gradient.reshape(ROWS, D))
    step_ratio = (rotated_moment / (jnp.sqrt(moment_two.reshape(NBLK, B, D)) + small_eps)).astype(jnp.bfloat16)
    unscaled_update = jnp.einsum('rfu,rup->rfp', broad_basis_matrix, step_ratio.astype(jnp.float32), precision=upper_limit)
    total = jnp.sum(unscaled_update * unscaled_update)
    scale = jnp.sqrt(jnp.float32(ROWS * D)) / (jnp.sqrt(total) + norm_eps)
    update = (unscaled_update * scale).reshape(ROWS, D).astype(jnp.bfloat16)
    return (update, moment_one, moment_two, basis_new)
```

```python
import functools
import jax
import jax.numpy as jnp
from jax import lax
from jax.experimental import pallas as pl
from jax.experimental.pallas import tpu as pltpu
from jax.sharding import PartitionSpec as P

beta_one = 0.9
beta_two = 0.95
small_eps = 1e-08
norm_eps = 1e-06
TILE = 256
HALF = 128


def split(value):
    high = value.astype(jnp.bfloat16)
    return high, (value - high.astype(jnp.float32)).astype(jnp.bfloat16)


def dot(left, right, across):
    return lax.dot_general(
        left, right, (((1,), (across,)), ((), ())), preferred_element_type=jnp.float32
    )


def dot3(left, right, across):
    left_high, left_low = left
    right_high, right_low = right
    return (
        dot(left_high, right_low, across)
        + dot(left_low, right_high, across)
        + dot(left_high, right_high, across)
    )


def inverse_factor(square):
    groups = HALF // 8
    rows = [square[8 * g : 8 * g + 8, :] for g in range(groups)]
    lane = lax.broadcasted_iota(jnp.int32, (8, HALF), 1)
    sub = lax.broadcasted_iota(jnp.int32, (8, HALF), 0)
    result = []
    for q in range(groups):
        first = 8 * q
        in_panel = (lane >= first) & (lane < first + 8)

        def columns(g):
            return [
                jnp.broadcast_to(rows[g][:, first + i : first + i + 1], (8, HALF)) for i in range(8)
            ]

        panel = columns(q)
        top = jnp.where(in_panel, jnp.where(lane - first == sub, 1.0, 0.0), rows[q])
        scale = jnp.zeros((8, HALF), jnp.float32)
        inverses, pivots, links = [], [], []
        for i in range(8):
            pivot = jnp.broadcast_to(panel[i][i : i + 1, :], (8, HALF))
            inverse = 1.0 / pivot
            factor = jnp.where(sub > i, panel[i] * inverse, 0.0)
            pivot_row = jnp.broadcast_to(top[i : i + 1, :], (8, HALF))
            link = {}
            for later in range(i + 1, 8):
                link[later] = jnp.broadcast_to(panel[later][i : i + 1, :], (8, HALF))
                panel[later] = panel[later] - factor * link[later]
            top = top - factor * pivot_row
            scale = jnp.where(sub == i, lax.rsqrt(pivot), scale)
            inverses.append(inverse)
            pivots.append(pivot_row)
            links.append(link)
        result.append(jnp.where(lane < first + 8, top * scale, 0.0))
        for g in range(q + 1, groups):
            below = columns(g)
            value = jnp.where(in_panel, 0.0, rows[g])
            for i in range(8):
                factor = below[i] * inverses[i]
                for later in range(i + 1, 8):
                    below[later] = below[later] - factor * links[i][later]
                value = value - factor * pivots[i]
            rows[g] = value
    return jnp.concatenate(result, axis=0)


def factor_kernel(
    count, gram_ref, inv_high, inv_low, low_high, low_low, diag_ref, side_ref, wide_high, wide_low
):
    def tile(index):
        return pl.ds(pl.multiple_of(index * TILE, TILE), TILE)

    def lower(i, k):
        return low_high[tile(i), tile(k)], low_low[tile(i), tile(k)]

    @pl.loop(0, count)
    def _(i):
        inv_high[tile(i), :] = jnp.zeros((TILE, count * TILE), jnp.bfloat16)
        inv_low[tile(i), :] = jnp.zeros((TILE, count * TILE), jnp.bfloat16)

    @pl.loop(0, count)
    def _(j):
        def column(i):
            def step(k, total):
                return total - dot3(lower(i, k), lower(j, k), 1)

            return lax.fori_loop(0, j, step, gram_ref[tile(i), tile(j)])

        diag_ref[...] = column(j)

        @pl.loop(0, 2)
        def _(h):
            part = pl.ds(pl.multiple_of(h * HALF, HALF), HALF)
            inverse = inverse_factor(diag_ref[part, part])
            high, low = split(inverse)
            wide_high[part, part] = high
            wide_low[part, part] = low

            @pl.when(h == 0)
            def _():
                side = dot3(split(diag_ref[HALF:, :HALF]), (high, low), 1)
                pair = split(side)
                side_ref[...] = side
                diag_ref[HALF:, HALF:] = diag_ref[HALF:, HALF:] - dot3(pair, pair, 1)
                wide_high[:HALF, HALF:] = jnp.zeros((HALF, HALF), jnp.bfloat16)
                wide_low[:HALF, HALF:] = jnp.zeros((HALF, HALF), jnp.bfloat16)

            @pl.when(h == 1)
            def _():
                first = wide_high[:HALF, :HALF], wide_low[:HALF, :HALF]
                corner = dot3(split(side_ref[...]), first, 0)
                corner_high, corner_low = split(-dot3((high, low), split(corner), 0))
                wide_high[HALF:, :HALF] = corner_high
                wide_low[HALF:, :HALF] = corner_low

        def wide():
            return wide_high[...], wide_low[...]

        @pl.loop(j + 1, count)
        def _(i):
            high, low = split(dot3(split(column(i)), wide(), 1))
            low_high[tile(i), tile(j)] = high
            low_low[tile(i), tile(j)] = low

        @pl.loop(0, j)
        def _(c):
            def step(k, total):
                return total + dot3(lower(j, k), (inv_high[tile(k), tile(c)], inv_low[tile(k), tile(c)]), 0)

            total = lax.fori_loop(c, j, step, jnp.zeros((TILE, TILE), jnp.float32))
            high, low = split(-dot3(wide(), split(total), 0))
            inv_high[tile(j), tile(c)] = high
            inv_low[tile(j), tile(c)] = low

        inv_high[tile(j), tile(j)] = wide_high[...]
        inv_low[tile(j), tile(j)] = wide_low[...]


def inverse_of_factor(gram):
    order = gram.shape[0]
    whole = jax.ShapeDtypeStruct((order, order), jnp.bfloat16)
    return pl.pallas_call(
        functools.partial(factor_kernel, order // TILE),
        out_shape=(whole, whole),
        in_specs=[pl.BlockSpec(memory_space=pltpu.VMEM)],
        out_specs=(pl.BlockSpec(memory_space=pltpu.VMEM), pl.BlockSpec(memory_space=pltpu.VMEM)),
        scratch_shapes=[
            pltpu.VMEM((order, order), jnp.bfloat16),
            pltpu.VMEM((order, order), jnp.bfloat16),
            pltpu.VMEM((TILE, TILE), jnp.float32),
            pltpu.VMEM((HALF, HALF), jnp.float32),
            pltpu.VMEM((TILE, TILE), jnp.bfloat16),
            pltpu.VMEM((TILE, TILE), jnp.bfloat16),
        ],
        compiler_params=pltpu.CompilerParams(vmem_limit_bytes=58 * 1024 * 1024),
    )(gram)


def rotate(rows, inverse):
    high, low = inverse
    return dot(rows, low, 1) + dot(rows, high, 1)


def on_device(precond, basis_old, gradient, moment_in, second_in):
    blocks = precond.shape[0]
    order = precond.shape[2]
    width = gradient.shape[1]
    power = jnp.einsum(
        "bik,bkj->bij",
        precond,
        lax.all_gather(basis_old, "fsdp", axis=1, tiled=True),
        preferred_element_type=jnp.float32,
    )
    power_half = power.astype(jnp.bfloat16)
    complete_power = lax.all_gather(power_half, "fsdp", axis=1, tiled=True)
    gram_sum = jnp.einsum(
        "bki,bkj->bij", complete_power, complete_power, preferred_element_type=jnp.float32
    )
    inverses = [inverse_of_factor(gram_sum[b]) for b in range(blocks)]
    basis_new = jnp.stack([rotate(power_half[b], inverses[b]) for b in range(blocks)])
    complete_basis = jnp.stack(
        [rotate(complete_power[b], inverses[b]).astype(jnp.bfloat16) for b in range(blocks)]
    )
    moment_one = beta_one * moment_in + (1.0 - beta_one) * gradient.astype(jnp.float32)
    moment_half = moment_one.astype(jnp.bfloat16)
    gradient_block_list = gradient.reshape(blocks, order, width)
    moment_block_list = moment_half.reshape(blocks, order, width)
    rotated_gradient = jnp.einsum(
        "aos,aol->asl", complete_basis, gradient_block_list, preferred_element_type=jnp.float32
    )
    rotated_moment = jnp.einsum(
        "aos,aol->asl", complete_basis, moment_block_list, preferred_element_type=jnp.float32
    )
    moment_two = beta_two * second_in.reshape(blocks, order, width) + (1.0 - beta_two) * jnp.square(
        rotated_gradient
    )
    step_ratio = (rotated_moment / (jnp.sqrt(moment_two) + small_eps)).astype(jnp.bfloat16)
    unscaled_update = jnp.einsum(
        "rfu,rup->rfp", complete_basis, step_ratio, preferred_element_type=jnp.float32
    )
    total = lax.psum(jnp.sum(unscaled_update * unscaled_update), ("owner", "fsdp"))
    count = gradient.shape[0] * lax.axis_size("owner") * width * lax.axis_size("fsdp")
    scale = jnp.sqrt(jnp.float32(count)) / (jnp.sqrt(total) + norm_eps)
    update = (unscaled_update * scale).reshape(blocks * order, width).astype(jnp.bfloat16)
    return (update, moment_one, moment_two.reshape(blocks * order, width), basis_new)


def solution(mesh):
    return jax.shard_map(
        on_device,
        mesh=mesh,
        in_specs=(
            P("owner", "fsdp", None),
            P("owner", "fsdp", None),
            P("owner", "fsdp"),
            P("owner", "fsdp"),
            P("owner", "fsdp"),
        ),
        out_specs=(
            P("owner", "fsdp"),
            P("owner", "fsdp"),
            P("owner", "fsdp"),
            P("owner", "fsdp", None),
        ),
        check_vma=False,
    )
```

```python
import functools
import jax
import jax.numpy as jnp
from jax import lax
from jax.experimental import pallas as pl
from jax.experimental.pallas import tpu as pltpu
from jax.sharding import PartitionSpec as P

beta_one = 0.9
beta_two = 0.95
small_eps = 1e-08
norm_eps = 1e-06
TILE = 256
HALF = 128


def split(value):
    high = value.astype(jnp.bfloat16)
    return high, (value - high.astype(jnp.float32)).astype(jnp.bfloat16)


def dot(left, right, across):
    return lax.dot_general(
        left, right, (((1,), (across,)), ((), ())), preferred_element_type=jnp.float32
    )


def dot3(left, right, across):
    left_high, left_low = left
    right_high, right_low = right
    return (
        dot(left_high, right_low, across)
        + dot(left_low, right_high, across)
        + dot(left_high, right_high, across)
    )


def inverse_factor(square):
    groups = HALF // 8
    rows = [square[8 * g : 8 * g + 8, :] for g in range(groups)]
    lane = lax.broadcasted_iota(jnp.int32, (8, HALF), 1)
    sub = lax.broadcasted_iota(jnp.int32, (8, HALF), 0)
    result = []
    for q in range(groups):
        first = 8 * q
        in_panel = (lane >= first) & (lane < first + 8)

        def columns(g):
            return [
                jnp.broadcast_to(rows[g][:, first + i : first + i + 1], (8, HALF)) for i in range(8)
            ]

        panel = columns(q)
        top = jnp.where(in_panel, jnp.where(lane - first == sub, 1.0, 0.0), rows[q])
        scale = jnp.zeros((8, HALF), jnp.float32)
        inverses, pivots, links = [], [], []
        for i in range(8):
            pivot = jnp.broadcast_to(panel[i][i : i + 1, :], (8, HALF))
            inverse = 1.0 / pivot
            factor = jnp.where(sub > i, panel[i] * inverse, 0.0)
            pivot_row = jnp.broadcast_to(top[i : i + 1, :], (8, HALF))
            link = {}
            for later in range(i + 1, 8):
                link[later] = jnp.broadcast_to(panel[later][i : i + 1, :], (8, HALF))
                panel[later] = panel[later] - factor * link[later]
            top = top - factor * pivot_row
            scale = jnp.where(sub == i, lax.rsqrt(pivot), scale)
            inverses.append(inverse)
            pivots.append(pivot_row)
            links.append(link)
        result.append(jnp.where(lane < first + 8, top * scale, 0.0))
        for g in range(q + 1, groups):
            below = columns(g)
            value = jnp.where(in_panel, 0.0, rows[g])
            for i in range(8):
                factor = below[i] * inverses[i]
                for later in range(i + 1, 8):
                    below[later] = below[later] - factor * links[i][later]
                value = value - factor * pivots[i]
            rows[g] = value
    return jnp.concatenate(result, axis=0)


def factor_kernel(
    count, gram_ref, inv_high, inv_low, low_high, low_low, diag_ref, side_ref, wide_high, wide_low
):
    def tile(index):
        return pl.ds(pl.multiple_of(index * TILE, TILE), TILE)

    def lower(i, k):
        return low_high[tile(i), tile(k)], low_low[tile(i), tile(k)]

    @pl.loop(0, count)
    def _(i):
        inv_high[tile(i), :] = jnp.zeros((TILE, count * TILE), jnp.bfloat16)
        inv_low[tile(i), :] = jnp.zeros((TILE, count * TILE), jnp.bfloat16)

    @pl.loop(0, count)
    def _(j):
        def column(i):
            def step(k, total):
                return total - dot3(lower(i, k), lower(j, k), 1)

            return lax.fori_loop(0, j, step, gram_ref[tile(i), tile(j)])

        diag_ref[...] = column(j)

        @pl.loop(0, 2)
        def _(h):
            part = pl.ds(pl.multiple_of(h * HALF, HALF), HALF)
            inverse = inverse_factor(diag_ref[part, part])
            high, low = split(inverse)
            wide_high[part, part] = high
            wide_low[part, part] = low

            @pl.when(h == 0)
            def _():
                side = dot3(split(diag_ref[HALF:, :HALF]), (high, low), 1)
                pair = split(side)
                side_ref[...] = side
                diag_ref[HALF:, HALF:] = diag_ref[HALF:, HALF:] - dot3(pair, pair, 1)
                wide_high[:HALF, HALF:] = jnp.zeros((HALF, HALF), jnp.bfloat16)
                wide_low[:HALF, HALF:] = jnp.zeros((HALF, HALF), jnp.bfloat16)

            @pl.when(h == 1)
            def _():
                first = wide_high[:HALF, :HALF], wide_low[:HALF, :HALF]
                corner = dot3(split(side_ref[...]), first, 0)
                corner_high, corner_low = split(-dot3((high, low), split(corner), 0))
                wide_high[HALF:, :HALF] = corner_high
                wide_low[HALF:, :HALF] = corner_low

        def wide():
            return wide_high[...], wide_low[...]

        @pl.loop(j + 1, count)
        def _(i):
            high, low = split(dot3(split(column(i)), wide(), 1))
            low_high[tile(i), tile(j)] = high
            low_low[tile(i), tile(j)] = low

        @pl.loop(0, j)
        def _(c):
            def step(k, total):
                return total + dot3(lower(j, k), (inv_high[tile(k), tile(c)], inv_low[tile(k), tile(c)]), 0)

            total = lax.fori_loop(c, j, step, jnp.zeros((TILE, TILE), jnp.float32))
            high, low = split(-dot3(wide(), split(total), 0))
            inv_high[tile(j), tile(c)] = high
            inv_low[tile(j), tile(c)] = low

        inv_high[tile(j), tile(j)] = wide_high[...]
        inv_low[tile(j), tile(j)] = wide_low[...]


def inverse_of_factor(gram):
    order = gram.shape[0]
    whole = jax.ShapeDtypeStruct((order, order), jnp.bfloat16)
    return pl.pallas_call(
        functools.partial(factor_kernel, order // TILE),
        out_shape=(whole, whole),
        in_specs=[pl.BlockSpec(memory_space=pltpu.VMEM)],
        out_specs=(pl.BlockSpec(memory_space=pltpu.VMEM), pl.BlockSpec(memory_space=pltpu.VMEM)),
        scratch_shapes=[
            pltpu.VMEM((order, order), jnp.bfloat16),
            pltpu.VMEM((order, order), jnp.bfloat16),
            pltpu.VMEM((TILE, TILE), jnp.float32),
            pltpu.VMEM((HALF, HALF), jnp.float32),
            pltpu.VMEM((TILE, TILE), jnp.bfloat16),
            pltpu.VMEM((TILE, TILE), jnp.bfloat16),
        ],
        compiler_params=pltpu.CompilerParams(vmem_limit_bytes=40 * 1024 * 1024),
        cost_estimate=pl.CostEstimate(
            flops=60 * order**3, bytes_accessed=8 * order**2, transcendentals=0
        ),
    )(gram)


def rotate(rows, inverse):
    high, low = inverse
    return dot(rows, low, 1) + dot(rows, high, 1)


def gram_of(left, right):
    return lax.dot_general(
        left, right, (((0,), (0,)), ((), ())), preferred_element_type=jnp.float32
    )


def refresh(factor, first_basis, second_basis, start, count):
    power_first = dot(factor, first_basis, 0).astype(jnp.bfloat16)
    inverse_first = inverse_of_factor(gram_of(power_first, power_first))
    basis_first = rotate(power_first, inverse_first).astype(jnp.bfloat16)
    inverse_first, basis_first, second_basis = lax.optimization_barrier(
        (inverse_first, basis_first, second_basis)
    )
    power_second = dot(factor, second_basis, 0).astype(jnp.bfloat16)
    side = split(dot3(split(gram_of(power_second, power_first)), inverse_first, 1))
    corner = gram_of(power_second, power_second) - dot3(side, side, 1)
    inverse_second = inverse_of_factor(corner)
    inverse_side = split(-dot3(inverse_second, split(dot3(side, inverse_first, 0)), 0))

    def second_columns(first_rows, second_rows):
        return rotate(first_rows, inverse_side) + rotate(second_rows, inverse_second)

    basis_second = second_columns(power_first, power_second).astype(jnp.bfloat16)
    own_first = lax.dynamic_slice_in_dim(power_first, start, count, 0)
    own_second = lax.dynamic_slice_in_dim(power_second, start, count, 0)
    own = [rotate(own_first, inverse_first), second_columns(own_first, own_second)]
    return jnp.concatenate(own, axis=1), jnp.concatenate([basis_first, basis_second], axis=1)


def sum_kernel(
    owners, shards, value_ref, total_ref, near, far, middle, near_sent, near_come, far_sent, far_come
):
    me_owner, me_shard = lax.axis_index("owner"), lax.axis_index("fsdp")

    def shard_at(step):
        return {"owner": me_owner, "fsdp": lax.rem(me_shard + step, shards)}

    def owner_at(step):
        return {"owner": lax.rem(me_owner + step, owners), "fsdp": me_shard}

    barrier = pltpu.get_barrier_semaphore()
    peers = [shard_at(step) for step in range(1, shards)]
    peers += [owner_at(step) for step in range(1, owners)]
    for peer in peers:
        pl.semaphore_signal(barrier, inc=1, device_id=peer, device_id_type=pl.DeviceIdType.MESH)
    pl.semaphore_wait(barrier, shards + owners - 2)

    def spread(source, boxes, sent, come, place, extent):
        copies = [
            pltpu.make_async_remote_copy(
                src_ref=source,
                dst_ref=boxes.at[step - 1],
                send_sem=sent.at[step - 1],
                recv_sem=come.at[step - 1],
                device_id=place(step),
                device_id_type=pl.DeviceIdType.MESH,
            )
            for step in range(1, extent)
        ]
        for copy in copies:
            copy.start()
        for copy in copies:
            copy.wait()
        total = source[...]
        for step in range(1, extent):
            total = total + boxes[step - 1]
        return total

    middle[...] = spread(value_ref, near, near_sent, near_come, shard_at, shards)
    total_ref[...] = spread(middle, far, far_sent, far_come, owner_at, owners)


def sum_everywhere(value):
    owners, shards = lax.axis_size("owner"), lax.axis_size("fsdp")
    shape = (8, 128)
    total = pl.pallas_call(
        functools.partial(sum_kernel, owners, shards),
        out_shape=jax.ShapeDtypeStruct(shape, jnp.float32),
        in_specs=[pl.BlockSpec(memory_space=pltpu.VMEM)],
        out_specs=pl.BlockSpec(memory_space=pltpu.VMEM),
        scratch_shapes=[
            pltpu.VMEM((shards - 1,) + shape, jnp.float32),
            pltpu.VMEM((owners - 1,) + shape, jnp.float32),
            pltpu.VMEM(shape, jnp.float32),
            pltpu.SemaphoreType.DMA((shards - 1,)),
            pltpu.SemaphoreType.DMA((shards - 1,)),
            pltpu.SemaphoreType.DMA((owners - 1,)),
            pltpu.SemaphoreType.DMA((owners - 1,)),
        ],
        compiler_params=pltpu.CompilerParams(collective_id=0, has_side_effects=True),
    )(jnp.broadcast_to(value, shape))
    return total[0, 0]


def on_device(precond, basis_old, gradient, moment_in, second_in):
    blocks, held, order = precond.shape
    width = gradient.shape[1]
    half = order // 2
    start = lax.axis_index("fsdp") * held
    factor = lax.all_gather(precond, "fsdp", axis=1, tiled=True)
    first_basis = lax.all_gather(basis_old[:, :, :half], "fsdp", axis=1, tiled=True)
    second_basis = lax.all_gather(basis_old[:, :, half:], "fsdp", axis=1, tiled=True)
    refreshed = [
        refresh(factor[b], first_basis[b], second_basis[b], start, held) for b in range(blocks)
    ]
    basis_new = jnp.stack([own for own, _ in refreshed])
    complete_basis = jnp.stack([whole for _, whole in refreshed])
    moment_one = beta_one * moment_in + (1.0 - beta_one) * gradient.astype(jnp.float32)
    moment_half = moment_one.astype(jnp.bfloat16)
    gradient_block_list = gradient.reshape(blocks, order, width)
    moment_block_list = moment_half.reshape(blocks, order, width)
    rotated_gradient = jnp.einsum(
        "aos,aol->asl", complete_basis, gradient_block_list, preferred_element_type=jnp.float32
    )
    rotated_moment = jnp.einsum(
        "aos,aol->asl", complete_basis, moment_block_list, preferred_element_type=jnp.float32
    )
    moment_two = beta_two * second_in.reshape(blocks, order, width) + (1.0 - beta_two) * jnp.square(
        rotated_gradient
    )
    step_ratio = (rotated_moment / (jnp.sqrt(moment_two) + small_eps)).astype(jnp.bfloat16)
    unscaled_update = jnp.einsum(
        "rfu,rup->rfp", complete_basis, step_ratio, preferred_element_type=jnp.float32
    )
    total = sum_everywhere(jnp.sum(unscaled_update * unscaled_update))
    count = gradient.shape[0] * lax.axis_size("owner") * width * lax.axis_size("fsdp")
    scale = jnp.sqrt(jnp.float32(count)) / (jnp.sqrt(total) + norm_eps)
    update = (unscaled_update * scale).reshape(blocks * order, width).astype(jnp.bfloat16)
    return (update, moment_one, moment_two.reshape(blocks * order, width), basis_new)


def solution(mesh):
    return jax.shard_map(
        on_device,
        mesh=mesh,
        in_specs=(
            P("owner", "fsdp", None),
            P("owner", "fsdp", None),
            P("owner", "fsdp"),
            P("owner", "fsdp"),
            P("owner", "fsdp"),
        ),
        out_specs=(
            P("owner", "fsdp"),
            P("owner", "fsdp"),
            P("owner", "fsdp"),
            P("owner", "fsdp", None),
        ),
        check_vma=False,
    )
```

```python
import functools
import jax
import jax.numpy as jnp
from jax import lax
from jax.experimental import pallas as pl
from jax.experimental.pallas import tpu as pltpu
from jax.sharding import PartitionSpec as P

beta_one = 0.9
beta_two = 0.95
small_eps = 1e-08
norm_eps = 1e-06
TILE = 256
HALF = 128


def split(value):
    high = value.astype(jnp.bfloat16)
    return high, (value - high.astype(jnp.float32)).astype(jnp.bfloat16)


def dot(left, right, across):
    return lax.dot_general(
        left, right, (((1,), (across,)), ((), ())), preferred_element_type=jnp.float32
    )


def dot3(left, right, across):
    left_high, left_low = left
    right_high, right_low = right
    return (
        dot(left_high, right_low, across)
        + dot(left_low, right_high, across)
        + dot(left_high, right_high, across)
    )


def inverse_factor(square):
    groups = HALF // 8
    rows = [square[8 * g : 8 * g + 8, :] for g in range(groups)]
    lane = lax.broadcasted_iota(jnp.int32, (8, HALF), 1)
    sub = lax.broadcasted_iota(jnp.int32, (8, HALF), 0)
    result = []
    for q in range(groups):
        first = 8 * q
        in_panel = (lane >= first) & (lane < first + 8)

        def columns(g):
            return [
                jnp.broadcast_to(rows[g][:, first + i : first + i + 1], (8, HALF)) for i in range(8)
            ]

        panel = columns(q)
        top = jnp.where(in_panel, jnp.where(lane - first == sub, 1.0, 0.0), rows[q])
        scale = jnp.zeros((8, HALF), jnp.float32)
        inverses, pivots, links = [], [], []
        for i in range(8):
            pivot = jnp.broadcast_to(panel[i][i : i + 1, :], (8, HALF))
            inverse = 1.0 / pivot
            factor = jnp.where(sub > i, panel[i] * inverse, 0.0)
            pivot_row = jnp.broadcast_to(top[i : i + 1, :], (8, HALF))
            link = {}
            for later in range(i + 1, 8):
                link[later] = jnp.broadcast_to(panel[later][i : i + 1, :], (8, HALF))
                panel[later] = panel[later] - factor * link[later]
            top = top - factor * pivot_row
            scale = jnp.where(sub == i, lax.rsqrt(pivot), scale)
            inverses.append(inverse)
            pivots.append(pivot_row)
            links.append(link)
        result.append(jnp.where(lane < first + 8, top * scale, 0.0))
        for g in range(q + 1, groups):
            below = columns(g)
            value = jnp.where(in_panel, 0.0, rows[g])
            for i in range(8):
                factor = below[i] * inverses[i]
                for later in range(i + 1, 8):
                    below[later] = below[later] - factor * links[i][later]
                value = value - factor * pivots[i]
            rows[g] = value
    return jnp.concatenate(result, axis=0)


def factor_kernel(
    count, gram_ref, inv_high, inv_low, low_high, low_low, diag_ref, side_ref, wide_high, wide_low
):
    def tile(index):
        return pl.ds(pl.multiple_of(index * TILE, TILE), TILE)

    def lower(i, k):
        return low_high[tile(i), tile(k)], low_low[tile(i), tile(k)]

    @pl.loop(0, count)
    def _(i):
        inv_high[tile(i), :] = jnp.zeros((TILE, count * TILE), jnp.bfloat16)
        inv_low[tile(i), :] = jnp.zeros((TILE, count * TILE), jnp.bfloat16)

    @pl.loop(0, count)
    def _(j):
        def column(i):
            def step(k, total):
                return total - dot3(lower(i, k), lower(j, k), 1)

            return lax.fori_loop(0, j, step, gram_ref[tile(i), tile(j)])

        diag_ref[...] = column(j)

        @pl.loop(0, 2)
        def _(h):
            part = pl.ds(pl.multiple_of(h * HALF, HALF), HALF)
            inverse = inverse_factor(diag_ref[part, part])
            high, low = split(inverse)
            wide_high[part, part] = high
            wide_low[part, part] = low

            @pl.when(h == 0)
            def _():
                side = dot3(split(diag_ref[HALF:, :HALF]), (high, low), 1)
                pair = split(side)
                side_ref[...] = side
                diag_ref[HALF:, HALF:] = diag_ref[HALF:, HALF:] - dot3(pair, pair, 1)
                wide_high[:HALF, HALF:] = jnp.zeros((HALF, HALF), jnp.bfloat16)
                wide_low[:HALF, HALF:] = jnp.zeros((HALF, HALF), jnp.bfloat16)

            @pl.when(h == 1)
            def _():
                first = wide_high[:HALF, :HALF], wide_low[:HALF, :HALF]
                corner = dot3(split(side_ref[...]), first, 0)
                corner_high, corner_low = split(-dot3((high, low), split(corner), 0))
                wide_high[HALF:, :HALF] = corner_high
                wide_low[HALF:, :HALF] = corner_low

        def wide():
            return wide_high[...], wide_low[...]

        @pl.loop(j + 1, count)
        def _(i):
            high, low = split(dot3(split(column(i)), wide(), 1))
            low_high[tile(i), tile(j)] = high
            low_low[tile(i), tile(j)] = low

        @pl.loop(0, j)
        def _(c):
            def step(k, total):
                return total + dot3(lower(j, k), (inv_high[tile(k), tile(c)], inv_low[tile(k), tile(c)]), 0)

            total = lax.fori_loop(c, j, step, jnp.zeros((TILE, TILE), jnp.float32))
            high, low = split(-dot3(wide(), split(total), 0))
            inv_high[tile(j), tile(c)] = high
            inv_low[tile(j), tile(c)] = low

        inv_high[tile(j), tile(j)] = wide_high[...]
        inv_low[tile(j), tile(j)] = wide_low[...]


def inverse_of_factor(gram):
    order = gram.shape[0]
    whole = jax.ShapeDtypeStruct((order, order), jnp.bfloat16)
    return pl.pallas_call(
        functools.partial(factor_kernel, order // TILE),
        out_shape=(whole, whole),
        in_specs=[pl.BlockSpec(memory_space=pltpu.VMEM)],
        out_specs=(pl.BlockSpec(memory_space=pltpu.VMEM), pl.BlockSpec(memory_space=pltpu.VMEM)),
        scratch_shapes=[
            pltpu.VMEM((order, order), jnp.bfloat16),
            pltpu.VMEM((order, order), jnp.bfloat16),
            pltpu.VMEM((TILE, TILE), jnp.float32),
            pltpu.VMEM((HALF, HALF), jnp.float32),
            pltpu.VMEM((TILE, TILE), jnp.bfloat16),
            pltpu.VMEM((TILE, TILE), jnp.bfloat16),
        ],
        compiler_params=pltpu.CompilerParams(vmem_limit_bytes=40 * 1024 * 1024),
        cost_estimate=pl.CostEstimate(
            flops=60 * order**3, bytes_accessed=8 * order**2, transcendentals=0
        ),
    )(gram)


def rotate(rows, inverse):
    high, low = inverse
    return dot(rows, low, 1) + dot(rows, high, 1)


def gram_of(left, right):
    return lax.dot_general(
        left, right, (((0,), (0,)), ((), ())), preferred_element_type=jnp.float32
    )


def refresh(factor, first_basis, second_basis, start, count):
    power_first = dot(factor, first_basis, 0).astype(jnp.bfloat16)
    inverse_first = inverse_of_factor(gram_of(power_first, power_first))
    basis_first = rotate(power_first, inverse_first).astype(jnp.bfloat16)
    inverse_first, basis_first, second_basis = lax.optimization_barrier(
        (inverse_first, basis_first, second_basis)
    )
    power_second = dot(factor, second_basis, 0).astype(jnp.bfloat16)
    side = split(dot3(split(gram_of(power_second, power_first)), inverse_first, 1))
    corner = gram_of(power_second, power_second) - dot3(side, side, 1)
    inverse_second = inverse_of_factor(corner)
    inverse_side = split(-dot3(inverse_second, split(dot3(side, inverse_first, 0)), 0))

    second = [
        jnp.concatenate(pair, axis=1) for pair in zip(inverse_side, inverse_second, strict=True)
    ]
    power = jnp.concatenate([power_first, power_second], axis=1)
    basis_second = rotate(power, second).astype(jnp.bfloat16)
    own_power = lax.dynamic_slice_in_dim(power, start, count, 0)
    own = [rotate(own_power[:, : power_first.shape[1]], inverse_first), rotate(own_power, second)]
    return jnp.concatenate(own, axis=1), jnp.concatenate([basis_first, basis_second], axis=1)


def symmetric_kernel(shards, sent_ref, whole_ref):
    held = whole_ref.shape[0] // shards

    def part(index):
        return pl.ds(pl.multiple_of(index * held, held), held)

    @pl.loop(0, shards)
    def _(i):
        for ahead in range(shards // 2 + 1):
            other = lax.rem(i + ahead, shards)
            block = sent_ref[part(i), ahead * held : (ahead + 1) * held]
            whole_ref[part(i), part(other)] = block
            if 0 < 2 * ahead < shards:
                whole_ref[part(other), part(i)] = block.T


def symmetric_whole(sent, shards):
    order = sent.shape[0]
    return pl.pallas_call(
        functools.partial(symmetric_kernel, shards),
        out_shape=jax.ShapeDtypeStruct((order, order), sent.dtype),
        in_specs=[pl.BlockSpec(memory_space=pltpu.VMEM)],
        out_specs=pl.BlockSpec(memory_space=pltpu.VMEM),
        compiler_params=pltpu.CompilerParams(vmem_limit_bytes=40 * 1024 * 1024),
    )(sent)


def sum_kernel(
    owners, shards, value_ref, total_ref, near, far, middle, near_sent, near_come, far_sent, far_come
):
    me_owner, me_shard = lax.axis_index("owner"), lax.axis_index("fsdp")

    def shard_at(step):
        return {"owner": me_owner, "fsdp": lax.rem(me_shard + step, shards)}

    def owner_at(step):
        return {"owner": lax.rem(me_owner + step, owners), "fsdp": me_shard}

    barrier = pltpu.get_barrier_semaphore()
    peers = [shard_at(step) for step in range(1, shards)]
    peers += [owner_at(step) for step in range(1, owners)]
    for peer in peers:
        pl.semaphore_signal(barrier, inc=1, device_id=peer, device_id_type=pl.DeviceIdType.MESH)
    pl.semaphore_wait(barrier, shards + owners - 2)

    def spread(source, boxes, sent, come, place, extent):
        copies = [
            pltpu.make_async_remote_copy(
                src_ref=source,
                dst_ref=boxes.at[step - 1],
                send_sem=sent.at[step - 1],
                recv_sem=come.at[step - 1],
                device_id=place(step),
                device_id_type=pl.DeviceIdType.MESH,
            )
            for step in range(1, extent)
        ]
        for copy in copies:
            copy.start()
        for copy in copies:
            copy.wait()
        total = source[...]
        for step in range(1, extent):
            total = total + boxes[step - 1]
        return total

    middle[...] = spread(value_ref, near, near_sent, near_come, shard_at, shards)
    total_ref[...] = spread(middle, far, far_sent, far_come, owner_at, owners)


def sum_everywhere(value):
    owners, shards = lax.axis_size("owner"), lax.axis_size("fsdp")
    shape = (8, 128)
    total = pl.pallas_call(
        functools.partial(sum_kernel, owners, shards),
        out_shape=jax.ShapeDtypeStruct(shape, jnp.float32),
        in_specs=[pl.BlockSpec(memory_space=pltpu.VMEM)],
        out_specs=pl.BlockSpec(memory_space=pltpu.VMEM),
        scratch_shapes=[
            pltpu.VMEM((shards - 1,) + shape, jnp.float32),
            pltpu.VMEM((owners - 1,) + shape, jnp.float32),
            pltpu.VMEM(shape, jnp.float32),
            pltpu.SemaphoreType.DMA((shards - 1,)),
            pltpu.SemaphoreType.DMA((shards - 1,)),
            pltpu.SemaphoreType.DMA((owners - 1,)),
            pltpu.SemaphoreType.DMA((owners - 1,)),
        ],
        compiler_params=pltpu.CompilerParams(collective_id=0, has_side_effects=True),
    )(jnp.broadcast_to(value, shape))
    return total[0, 0]


def on_device(precond, basis_old, gradient, moment_in, second_in):
    blocks, held, order = precond.shape
    width = gradient.shape[1]
    half = order // 2
    start = lax.axis_index("fsdp") * held
    shards = lax.axis_size("fsdp")
    sent = held * (shards // 2 + 1)
    ahead = lax.dynamic_slice_in_dim(
        jnp.concatenate([precond, precond[:, :, :sent]], axis=2), start, sent, 2
    )
    gathered = lax.all_gather(
        jnp.concatenate([ahead, basis_old[:, :, :half]], axis=2), "fsdp", axis=1, tiled=True
    )
    factor = [symmetric_whole(gathered[b], shards) for b in range(blocks)]
    first_basis = gathered[:, :, sent:]
    second_basis = lax.all_gather(basis_old[:, :, half:], "fsdp", axis=1, tiled=True)
    refreshed = [
        refresh(factor[b], first_basis[b], second_basis[b], start, held) for b in range(blocks)
    ]
    basis_new = jnp.stack([own for own, _ in refreshed])
    complete_basis = jnp.stack([whole for _, whole in refreshed])
    moment_one = beta_one * moment_in + (1.0 - beta_one) * gradient.astype(jnp.float32)
    moment_half = moment_one.astype(jnp.bfloat16)
    gradient_block_list = gradient.reshape(blocks, order, width)
    moment_block_list = moment_half.reshape(blocks, order, width)
    rotated_gradient = jnp.einsum(
        "aos,aol->asl", complete_basis, gradient_block_list, preferred_element_type=jnp.float32
    )
    rotated_moment = jnp.einsum(
        "aos,aol->asl", complete_basis, moment_block_list, preferred_element_type=jnp.float32
    )
    moment_two = beta_two * second_in.reshape(blocks, order, width) + (1.0 - beta_two) * jnp.square(
        rotated_gradient
    )
    step_ratio = (rotated_moment / (jnp.sqrt(moment_two) + small_eps)).astype(jnp.bfloat16)
    unscaled_update = jnp.einsum(
        "rfu,rup->rfp", complete_basis, step_ratio, preferred_element_type=jnp.float32
    )
    total = sum_everywhere(jnp.sum(unscaled_update * unscaled_update))
    count = gradient.shape[0] * lax.axis_size("owner") * width * lax.axis_size("fsdp")
    scale = jnp.sqrt(jnp.float32(count)) / (jnp.sqrt(total) + norm_eps)
    update = (unscaled_update * scale).reshape(blocks * order, width).astype(jnp.bfloat16)
    return (update, moment_one, moment_two.reshape(blocks * order, width), basis_new)


def solution(mesh):
    return jax.shard_map(
        on_device,
        mesh=mesh,
        in_specs=(
            P("owner", "fsdp", None),
            P("owner", "fsdp", None),
            P("owner", "fsdp"),
            P("owner", "fsdp"),
            P("owner", "fsdp"),
        ),
        out_specs=(
            P("owner", "fsdp"),
            P("owner", "fsdp"),
            P("owner", "fsdp"),
            P("owner", "fsdp", None),
        ),
        check_vma=False,
    )
```

```python
import functools
import jax
import jax.numpy as jnp
from jax import lax
from jax.experimental import pallas as pl
from jax.experimental.pallas import tpu as pltpu
from jax.sharding import PartitionSpec as P

beta_one = 0.9
beta_two = 0.95
small_eps = 1e-08
norm_eps = 1e-06
TILE = 256
HALF = 128


def split(value):
    high = value.astype(jnp.bfloat16)
    return high, (value - high.astype(jnp.float32)).astype(jnp.bfloat16)


def dot(left, right, across):
    return lax.dot_general(
        left, right, (((1,), (across,)), ((), ())), preferred_element_type=jnp.float32
    )


def dot3(left, right, across):
    left_high, left_low = left
    right_high, right_low = right
    return (
        dot(left_high, right_low, across)
        + dot(left_low, right_high, across)
        + dot(left_high, right_high, across)
    )


def inverse_factor(square):
    groups = HALF // 8
    rows = [square[8 * g : 8 * g + 8, :] for g in range(groups)]
    lane = lax.broadcasted_iota(jnp.int32, (8, HALF), 1)
    sub = lax.broadcasted_iota(jnp.int32, (8, HALF), 0)
    result = []
    for q in range(groups):
        first = 8 * q
        in_panel = (lane >= first) & (lane < first + 8)

        def columns(g):
            return [
                jnp.broadcast_to(rows[g][:, first + i : first + i + 1], (8, HALF)) for i in range(8)
            ]

        panel = columns(q)
        top = jnp.where(in_panel, jnp.where(lane - first == sub, 1.0, 0.0), rows[q])
        scale = jnp.zeros((8, HALF), jnp.float32)
        inverses, pivots, links = [], [], []
        for i in range(8):
            pivot = jnp.broadcast_to(panel[i][i : i + 1, :], (8, HALF))
            inverse = 1.0 / pivot
            factor = jnp.where(sub > i, panel[i] * inverse, 0.0)
            pivot_row = jnp.broadcast_to(top[i : i + 1, :], (8, HALF))
            link = {}
            for later in range(i + 1, 8):
                link[later] = jnp.broadcast_to(panel[later][i : i + 1, :], (8, HALF))
                panel[later] = panel[later] - factor * link[later]
            top = top - factor * pivot_row
            scale = jnp.where(sub == i, lax.rsqrt(pivot), scale)
            inverses.append(inverse)
            pivots.append(pivot_row)
            links.append(link)
        result.append(jnp.where(lane < first + 8, top * scale, 0.0))
        for g in range(q + 1, groups):
            below = columns(g)
            value = jnp.where(in_panel, 0.0, rows[g])
            for i in range(8):
                factor = below[i] * inverses[i]
                for later in range(i + 1, 8):
                    below[later] = below[later] - factor * links[i][later]
                value = value - factor * pivots[i]
            rows[g] = value
    return jnp.concatenate(result, axis=0)


def factor_kernel(
    count, gram_ref, inv_high, inv_low, low_high, low_low, diag_ref, side_ref, wide_high, wide_low
):
    def tile(index):
        return pl.ds(pl.multiple_of(index * TILE, TILE), TILE)

    def lower(i, k):
        return low_high[tile(i), tile(k)], low_low[tile(i), tile(k)]

    @pl.loop(0, count)
    def _(i):
        inv_high[tile(i), :] = jnp.zeros((TILE, count * TILE), jnp.bfloat16)
        inv_low[tile(i), :] = jnp.zeros((TILE, count * TILE), jnp.bfloat16)

    @pl.loop(0, count)
    def _(j):
        def column(i):
            def step(k, total):
                return total - dot3(lower(i, k), lower(j, k), 1)

            return lax.fori_loop(0, j, step, gram_ref[tile(i), tile(j)])

        diag_ref[...] = column(j)

        @pl.loop(0, 2)
        def _(h):
            part = pl.ds(pl.multiple_of(h * HALF, HALF), HALF)
            inverse = inverse_factor(diag_ref[part, part])
            high, low = split(inverse)
            wide_high[part, part] = high
            wide_low[part, part] = low

            @pl.when(h == 0)
            def _():
                side = dot3(split(diag_ref[HALF:, :HALF]), (high, low), 1)
                pair = split(side)
                side_ref[...] = side
                diag_ref[HALF:, HALF:] = diag_ref[HALF:, HALF:] - dot3(pair, pair, 1)
                wide_high[:HALF, HALF:] = jnp.zeros((HALF, HALF), jnp.bfloat16)
                wide_low[:HALF, HALF:] = jnp.zeros((HALF, HALF), jnp.bfloat16)

            @pl.when(h == 1)
            def _():
                first = wide_high[:HALF, :HALF], wide_low[:HALF, :HALF]
                corner = dot3(split(side_ref[...]), first, 0)
                corner_high, corner_low = split(-dot3((high, low), split(corner), 0))
                wide_high[HALF:, :HALF] = corner_high
                wide_low[HALF:, :HALF] = corner_low

        def wide():
            return wide_high[...], wide_low[...]

        @pl.loop(j + 1, count)
        def _(i):
            high, low = split(dot3(split(column(i)), wide(), 1))
            low_high[tile(i), tile(j)] = high
            low_low[tile(i), tile(j)] = low

        @pl.loop(0, j)
        def _(c):
            def step(k, total):
                return total + dot3(lower(j, k), (inv_high[tile(k), tile(c)], inv_low[tile(k), tile(c)]), 0)

            total = lax.fori_loop(c, j, step, jnp.zeros((TILE, TILE), jnp.float32))
            high, low = split(-dot3(wide(), split(total), 0))
            inv_high[tile(j), tile(c)] = high
            inv_low[tile(j), tile(c)] = low

        inv_high[tile(j), tile(j)] = wide_high[...]
        inv_low[tile(j), tile(j)] = wide_low[...]


def inverse_of_factor(gram):
    order = gram.shape[0]
    whole = jax.ShapeDtypeStruct((order, order), jnp.bfloat16)
    return pl.pallas_call(
        functools.partial(factor_kernel, order // TILE),
        out_shape=(whole, whole),
        in_specs=[pl.BlockSpec(memory_space=pltpu.VMEM)],
        out_specs=(pl.BlockSpec(memory_space=pltpu.VMEM), pl.BlockSpec(memory_space=pltpu.VMEM)),
        scratch_shapes=[
            pltpu.VMEM((order, order), jnp.bfloat16),
            pltpu.VMEM((order, order), jnp.bfloat16),
            pltpu.VMEM((TILE, TILE), jnp.float32),
            pltpu.VMEM((HALF, HALF), jnp.float32),
            pltpu.VMEM((TILE, TILE), jnp.bfloat16),
            pltpu.VMEM((TILE, TILE), jnp.bfloat16),
        ],
        compiler_params=pltpu.CompilerParams(vmem_limit_bytes=40 * 1024 * 1024),
        cost_estimate=pl.CostEstimate(
            flops=60 * order**3, bytes_accessed=8 * order**2, transcendentals=0
        ),
    )(gram)


def rotate(rows, inverse):
    high, low = inverse
    return dot(rows, low, 1) + dot(rows, high, 1)


def gram_of(left, right):
    return lax.dot_general(
        left, right, (((0,), (0,)), ((), ())), preferred_element_type=jnp.float32
    )


def refresh(factor, first_basis, second_basis, start, count):
    power_first = dot(factor, first_basis, 0).astype(jnp.bfloat16)
    inverse_first = inverse_of_factor(gram_of(power_first, power_first))
    basis_first = rotate(power_first, inverse_first).astype(jnp.bfloat16)
    inverse_first, basis_first, second_basis = lax.optimization_barrier(
        (inverse_first, basis_first, second_basis)
    )
    power_second = dot(factor, second_basis, 0).astype(jnp.bfloat16)
    side = split(dot3(split(gram_of(power_second, power_first)), inverse_first, 1))
    corner = gram_of(power_second, power_second) - dot3(side, side, 1)
    inverse_second = inverse_of_factor(corner)
    inverse_side = split(-dot3(inverse_second, split(dot3(side, inverse_first, 0)), 0))

    second = [
        jnp.concatenate(pair, axis=1) for pair in zip(inverse_side, inverse_second, strict=True)
    ]
    power = lax.optimization_barrier(jnp.concatenate([power_first, power_second], axis=1))
    basis_second = rotate(power, second).astype(jnp.bfloat16)
    own_power = lax.dynamic_slice_in_dim(power, start, count, 0)
    own = [rotate(own_power[:, : power_first.shape[1]], inverse_first), rotate(own_power, second)]
    return jnp.concatenate(own, axis=1), jnp.concatenate([basis_first, basis_second], axis=1)


def symmetric_kernel(shards, sent_ref, whole_ref):
    held = whole_ref.shape[0] // shards

    def part(index):
        return pl.ds(pl.multiple_of(index * held, held), held)

    @pl.loop(0, shards)
    def _(i):
        for ahead in range(shards // 2 + 1):
            other = lax.rem(i + ahead, shards)
            block = sent_ref[part(i), ahead * held : (ahead + 1) * held]
            whole_ref[part(i), part(other)] = block
            if 0 < 2 * ahead < shards:
                whole_ref[part(other), part(i)] = block.T


def symmetric_whole(sent, shards):
    order = sent.shape[0]
    return pl.pallas_call(
        functools.partial(symmetric_kernel, shards),
        out_shape=jax.ShapeDtypeStruct((order, order), sent.dtype),
        in_specs=[pl.BlockSpec(memory_space=pltpu.VMEM)],
        out_specs=pl.BlockSpec(memory_space=pltpu.VMEM),
        compiler_params=pltpu.CompilerParams(vmem_limit_bytes=40 * 1024 * 1024),
    )(sent)


def sum_kernel(
    owners, shards, value_ref, total_ref, near, far, middle, near_sent, near_come, far_sent, far_come
):
    me_owner, me_shard = lax.axis_index("owner"), lax.axis_index("fsdp")

    def shard_at(step):
        return {"owner": me_owner, "fsdp": lax.rem(me_shard + step, shards)}

    def owner_at(step):
        return {"owner": lax.rem(me_owner + step, owners), "fsdp": me_shard}

    barrier = pltpu.get_barrier_semaphore()
    peers = [shard_at(step) for step in range(1, shards)]
    peers += [owner_at(step) for step in range(1, owners)]
    for peer in peers:
        pl.semaphore_signal(barrier, inc=1, device_id=peer, device_id_type=pl.DeviceIdType.MESH)
    pl.semaphore_wait(barrier, shards + owners - 2)

    def spread(source, boxes, sent, come, place, extent):
        copies = [
            pltpu.make_async_remote_copy(
                src_ref=source,
                dst_ref=boxes.at[step - 1],
                send_sem=sent.at[step - 1],
                recv_sem=come.at[step - 1],
                device_id=place(step),
                device_id_type=pl.DeviceIdType.MESH,
            )
            for step in range(1, extent)
        ]
        for copy in copies:
            copy.start()
        for copy in copies:
            copy.wait()
        total = source[...]
        for step in range(1, extent):
            total = total + boxes[step - 1]
        return total

    middle[...] = spread(value_ref, near, near_sent, near_come, shard_at, shards)
    total_ref[...] = spread(middle, far, far_sent, far_come, owner_at, owners)


def sum_everywhere(value):
    owners, shards = lax.axis_size("owner"), lax.axis_size("fsdp")
    shape = (8, 128)
    total = pl.pallas_call(
        functools.partial(sum_kernel, owners, shards),
        out_shape=jax.ShapeDtypeStruct(shape, jnp.float32),
        in_specs=[pl.BlockSpec(memory_space=pltpu.VMEM)],
        out_specs=pl.BlockSpec(memory_space=pltpu.VMEM),
        scratch_shapes=[
            pltpu.VMEM((shards - 1,) + shape, jnp.float32),
            pltpu.VMEM((owners - 1,) + shape, jnp.float32),
            pltpu.VMEM(shape, jnp.float32),
            pltpu.SemaphoreType.DMA((shards - 1,)),
            pltpu.SemaphoreType.DMA((shards - 1,)),
            pltpu.SemaphoreType.DMA((owners - 1,)),
            pltpu.SemaphoreType.DMA((owners - 1,)),
        ],
        compiler_params=pltpu.CompilerParams(collective_id=0, has_side_effects=True),
    )(jnp.broadcast_to(value, shape))
    return total[0, 0]


def on_device(precond, basis_old, gradient, moment_in, second_in):
    blocks, held, order = precond.shape
    width = gradient.shape[1]
    half = order // 2
    start = lax.axis_index("fsdp") * held
    shards = lax.axis_size("fsdp")
    sent = held * (shards // 2 + 1)
    ahead = lax.dynamic_slice_in_dim(
        jnp.concatenate([precond, precond[:, :, :sent]], axis=2), start, sent, 2
    )
    gathered = lax.all_gather(
        jnp.concatenate([ahead, basis_old[:, :, :half]], axis=2), "fsdp", axis=1, tiled=True
    )
    factor = [symmetric_whole(gathered[b], shards) for b in range(blocks)]
    first_basis = gathered[:, :, sent:]
    second_basis = lax.all_gather(basis_old[:, :, half:], "fsdp", axis=1, tiled=True)
    refreshed = [
        refresh(factor[b], first_basis[b], second_basis[b], start, held) for b in range(blocks)
    ]
    basis_new = jnp.stack([own for own, _ in refreshed])
    complete_basis = jnp.stack([whole for _, whole in refreshed])
    moment_one = beta_one * moment_in + (1.0 - beta_one) * gradient.astype(jnp.float32)
    moment_half = moment_one.astype(jnp.bfloat16)
    gradient_block_list = gradient.reshape(blocks, order, width)
    moment_block_list = moment_half.reshape(blocks, order, width)
    rotated_gradient = jnp.einsum(
        "aos,aol->asl", complete_basis, gradient_block_list, preferred_element_type=jnp.float32
    )
    rotated_moment = jnp.einsum(
        "aos,aol->asl", complete_basis, moment_block_list, preferred_element_type=jnp.float32
    )
    moment_two = beta_two * second_in.reshape(blocks, order, width) + (1.0 - beta_two) * jnp.square(
        rotated_gradient
    )
    step_ratio = (rotated_moment / (jnp.sqrt(moment_two) + small_eps)).astype(jnp.bfloat16)
    unscaled_update = jnp.einsum(
        "rfu,rup->rfp", complete_basis, step_ratio, preferred_element_type=jnp.float32
    )
    total = sum_everywhere(jnp.sum(unscaled_update * unscaled_update))
    count = gradient.shape[0] * lax.axis_size("owner") * width * lax.axis_size("fsdp")
    scale = jnp.sqrt(jnp.float32(count)) / (jnp.sqrt(total) + norm_eps)
    update = (unscaled_update * scale).reshape(blocks * order, width).astype(jnp.bfloat16)
    return (update, moment_one, moment_two.reshape(blocks * order, width), basis_new)


def solution(mesh):
    return jax.shard_map(
        on_device,
        mesh=mesh,
        in_specs=(
            P("owner", "fsdp", None),
            P("owner", "fsdp", None),
            P("owner", "fsdp"),
            P("owner", "fsdp"),
            P("owner", "fsdp"),
        ),
        out_specs=(
            P("owner", "fsdp"),
            P("owner", "fsdp"),
            P("owner", "fsdp"),
            P("owner", "fsdp", None),
        ),
        check_vma=False,
    )
```
